32 devices in a mesh: groups: 2 (over x), hours: 8 (over z, y), units: 2 (over core).
Axes of the slice: x: 2, y: 2, z: 4, core: 2. Of those that a mesh axis runs over, the one named last changes fastest.
Arguments:
- unit_zone: int32 [1024], P('units'), may hold values from 0 to 63
- up_window: int32 [1024], P('units'), may hold values from 1 to 24
- down_window: int32 [1024], P('units'), may hold values from 1 to 24
- switchable: int32 [1024], P('units'), may hold values 0 or 1
- capacity: float32 [1024], P('units'), may hold values from 0.5 to 2
- fixed_cost: float32 [1024], P('units'), may hold values from 0.1 to 1
- start_cost: float32 [1024], P('units'), may hold values from 0.5 to 8
- fuel_cost: float32 [2048, 1024], P(('groups', 'units'), 'hours'), parts along dimension 0, may hold values from 0.3 to 3
- demand: float32 [128, 1024], P('groups', 'hours'), parts along dimension 0, may hold values from 15 to 35
- commit: float32 [2048, 1024], P(('groups', 'units'), 'hours'), parts along dimension 0, may hold values from 0 to 1
- output: float32 [2048, 1024], P(('groups', 'units'), 'hours'), parts along dimension 0, may hold values from 0 to 1.5
- startup: float32 [2048, 1024], P(('groups', 'units'), 'hours'), parts along dimension 0, may hold values from 0 to 0.3
- price: float32 [128, 1024], P('groups', 'hours'), parts along dimension 0, may hold values from -6 to 6
- link_dual: float32 [2048, 1024], P(('groups', 'units'), 'hours'), parts along dimension 0, may hold values from 0 to 1
- up_dual: float32 [2048, 1024], P(('groups', 'units'), 'hours'), parts along dimension 0, may hold values from 0 to 1
- down_dual: float32 [2048, 1024], P(('groups', 'units'), 'hours'), parts along dimension 0, may hold values from 0 to 1
Outputs:
- commit_out: float32 [2048, 1024], P(('groups', 'units'), 'hours'), parts along dimension 0
- output_out: float32 [2048, 1024], P(('groups', 'units'), 'hours'), parts along dimension 0
- startup_out: float32 [2048, 1024], P(('groups', 'units'), 'hours'), parts along dimension 0
- price_out: float32 [128, 1024], P('groups', 'hours'), parts along dimension 0
- link_out: float32 [2048, 1024], P(('groups', 'units'), 'hours'), parts along dimension 0
- up_out: float32 [2048, 1024], P(('groups', 'units'), 'hours'), parts along dimension 0
- down_out: float32 [2048, 1024], P(('groups', 'units'), 'hours'), parts along dimension 0
The draws below stay inside these ranges and needn't reach their ends.
There are 2 independent parts, one for each index of `groups`. The reference program is written for one: setup_inputs(seed, part) draws one part's arguments, and reference() takes and returns one part's arrays. A program takes and returns all parts, laid end to end along the dimension named above; an argument that names none is the same for every part. Nothing has to cross between parts.
All inputs are finite; a program needn't handle non-finite values. No bound on the sum of `switchable` on one device may be relied on, other than what follows from the above.
Results may differ from the reference program's by a relative error of at most 0.0003.
Values sent between devices are 32-bit elements; how exact they have to be, the bound alone decides.
A program may use at most 64 MiB of HBM per device.

```python
import math
import jax
import jax.numpy as jnp
from jax import lax

Z = 64
WIN = 24
UNITS = 1024
HOURS = 1024


def place_ends(entries, stream_key, least, largest):
    spot = [jax.random.randint(jax.random.fold_in(stream_key, axis), (), 0, length) for axis, length in enumerate(entries.shape)]
    main_axis = entries.shape.index(max(entries.shape))
    next_to = spot[:main_axis] + [(spot[main_axis] + 1) % entries.shape[main_axis]] + spot[main_axis + 1:]
    return entries.at[tuple(spot)].set(least).at[tuple(next_to)].set(largest)


def block_levels(own_key, shape, pieces, low, top_value):
    level, own = 1.0, jax.random.fold_in(own_key, 6)
    for position, blocks in pieces:
        steps = jnp.exp(jax.random.uniform(jax.random.fold_in(own, position), (blocks,), jnp.float32, low / len(pieces), top_value / len(pieces)))
        level = level * jnp.repeat(steps, shape[position] // blocks).reshape([-1 if axis == position else 1 for axis in range(len(shape))])
    return level


def normal_values(stream_key, dims, width, most, pieces=(), held_as=jnp.bfloat16):
    array = width * jax.random.normal(stream_key, dims, jnp.float32)
    if pieces:
        array = array * block_levels(stream_key, dims, pieces, -0.22, 0.18)
    return jnp.clip(array, -most, most).astype(held_as)


def setup_inputs(seed: int = 0, part: int = 0) -> dict:
    key_of = jax.random.split(jax.random.key(seed), 17)
    part_keys = jax.random.split(jax.random.fold_in(key_of[16], part), 17)
    unit_zone = place_ends(jax.random.randint(key_of[0], (UNITS,), 0, Z), jax.random.fold_in(key_of[0], 1), 0, Z - 1).astype(jnp.int32)
    up_window = place_ends(jax.random.randint(key_of[1], (UNITS,), 1, WIN + 1), jax.random.fold_in(key_of[1], 1), 1, WIN).astype(jnp.int32)
    down_window = place_ends(jax.random.randint(key_of[2], (UNITS,), 1, WIN + 1), jax.random.fold_in(key_of[2], 1), 1, WIN).astype(jnp.int32)
    switchable = place_ends((jax.random.randint(key_of[3], (UNITS,), 0, 4) < 3).astype(jnp.int32), jax.random.fold_in(key_of[3], 1), 0, 1)
    capacity = jnp.clip(jnp.exp(math.log(2.0) - 1.3862944 * jax.random.uniform(key_of[4], (UNITS,), jnp.float32) ** block_levels(key_of[4], (UNITS,), ((0, 2),), -0.2, 0.2)), 0.5, 2.0)
    fixed_cost = jnp.clip(0.1 + 0.9 * jax.random.uniform(key_of[5], (UNITS,), jnp.float32) ** block_levels(key_of[5], (UNITS,), ((0, 2),), -0.2, 0.2), 0.1, 1.0)
    start_cost = jnp.clip(jnp.exp(math.log(8.0) - 2.7725887 * jax.random.uniform(key_of[6], (UNITS,), jnp.float32) ** block_levels(key_of[6], (UNITS,), ((0, 2),), -0.2, 0.2)), 0.5, 8.0)
    fuel_cost = jnp.clip(jnp.exp(math.log(3.0) - 2.3025851 * jax.random.uniform(part_keys[7], (UNITS, HOURS), jnp.float32) ** block_levels(part_keys[7], (UNITS, HOURS), ((0, 2), (1, 8)), -0.2, 0.2)), 0.3, 3.0)
    demand = jnp.clip(15.0 + 20.0 * jax.random.uniform(part_keys[8], (Z, HOURS), jnp.float32) ** block_levels(part_keys[8], (Z, HOURS), ((1, 8),), -0.2, 0.2), 15.0, 35.0)
    commit = jnp.clip(1.0 * jax.random.uniform(part_keys[9], (UNITS, HOURS), jnp.float32) ** block_levels(part_keys[9], (UNITS, HOURS), ((0, 2), (1, 8)), -0.2, 0.2), 0.0, 1.0)
    output = jnp.clip(1.5 * jax.random.uniform(part_keys[10], (UNITS, HOURS), jnp.float32) ** block_levels(part_keys[10], (UNITS, HOURS), ((0, 2), (1, 8)), -0.2, 0.2), 0.0, 1.5)
    startup = jnp.clip(0.3 * jax.random.uniform(part_keys[11], (UNITS, HOURS), jnp.float32) ** block_levels(part_keys[11], (UNITS, HOURS), ((0, 2), (1, 8)), -0.2, 0.2), 0.0, 0.3)
    price = normal_values(part_keys[12], (Z, HOURS), 1.0, 6.0, ((1, 8),), jnp.float32)
    link_dual = jnp.clip(1.0 * jax.random.uniform(part_keys[13], (UNITS, HOURS), jnp.float32) ** block_levels(part_keys[13], (UNITS, HOURS), ((0, 2), (1, 8)), -0.2, 0.2), 0.0, 1.0)
    up_dual = jnp.clip(1.0 * jax.random.uniform(part_keys[14], (UNITS, HOURS), jnp.float32) ** block_levels(part_keys[14], (UNITS, HOURS), ((0, 2), (1, 8)), -0.2, 0.2), 0.0, 1.0)
    down_dual = jnp.clip(1.0 * jax.random.uniform(part_keys[15], (UNITS, HOURS), jnp.float32) ** block_levels(part_keys[15], (UNITS, HOURS), ((0, 2), (1, 8)), -0.2, 0.2), 0.0, 1.0)
    return dict(unit_zone=unit_zone, up_window=up_window, down_window=down_window, switchable=switchable, capacity=capacity, fixed_cost=fixed_cost, start_cost=start_cost, fuel_cost=fuel_cost, demand=demand, commit=commit, output=output, startup=startup, price=price, link_dual=link_dual, up_dual=up_dual, down_dual=down_dual)


step_scale = 0.015
epsilon = 1e-06

def project_segment(point_x, point_g, start_x, start_g, end_x, end_g):
    delta_x = end_x - start_x
    delta_g = end_g - start_g
    length = delta_x * delta_x + delta_g * delta_g
    along = (point_x - start_x) * delta_x + (point_g - start_g) * delta_g
    ratio = jnp.where(length > 0, along / jnp.where(length > 0, length, 1.0), 0.0)
    ratio = jnp.clip(ratio, 0.0, 1.0)
    near_x = start_x + ratio * delta_x
    near_g = start_g + ratio * delta_g
    gap_x = point_x - near_x
    gap_g = point_g - near_g
    return (near_x, near_g, gap_x * gap_x + gap_g * gap_g)

def project_pair(point_x, point_g, floor_commit, limit):
    zero = jnp.zeros_like(limit)
    unity = jnp.ones_like(limit)
    corners = ((floor_commit, zero), (unity, zero), (unity, limit), (floor_commit, limit * floor_commit))
    best_x, best_g, best_d = project_segment(point_x, point_g, corners[0][0], corners[0][1], corners[1][0], corners[1][1])
    for side in range(1, 4):
        other = corners[(side + 1) % 4]
        nearer_x, nearer_g, distance = project_segment(point_x, point_g, corners[side][0], corners[side][1], other[0], other[1])
        closer = distance < best_d
        best_x = jnp.where(closer, nearer_x, best_x)
        best_g = jnp.where(closer, nearer_g, best_g)
        best_d = jnp.where(closer, distance, best_d)
    inside = (point_x >= floor_commit) & (point_x <= 1.0) & (point_g >= 0.0) & (point_g <= limit * point_x)
    return (jnp.where(inside, point_x, best_x), jnp.where(inside, point_g, best_g))

def constraint_rows(commit, startup, up_window, down_window):
    up_sum = jnp.zeros_like(commit)
    down_sum = jnp.zeros_like(commit)
    lagged = jnp.zeros_like(commit)
    for offset in range(WIN):
        moved = jnp.roll(startup, offset, axis=1)
        up_sum = up_sum + jnp.where(offset < up_window[:, None], moved, 0.0)
        down_sum = down_sum + jnp.where(offset < down_window[:, None], moved, 0.0)
        lagged = lagged + jnp.where(down_window[:, None] == offset + 1, jnp.roll(commit, offset + 1, axis=1), 0.0)
    link = commit - jnp.roll(commit, 1, axis=1) - startup
    upper = up_sum - commit
    lower = down_sum + lagged - 1.0
    return (link, upper, lower)

def adjoint_terms(link_dual, up_dual, down_dual, up_window, down_window):
    grad_commit = link_dual - jnp.roll(link_dual, -1, axis=1) - up_dual
    grad_startup = -link_dual
    for offset in range(WIN):
        grad_startup = grad_startup + jnp.where(offset < up_window[:, None], jnp.roll(up_dual, -offset, axis=1), 0.0)
        grad_startup = grad_startup + jnp.where(offset < down_window[:, None], jnp.roll(down_dual, -offset, axis=1), 0.0)
        grad_commit = grad_commit + jnp.where(down_window[:, None] == offset + 1, jnp.roll(down_dual, -offset - 1, axis=1), 0.0)
    return (grad_commit, grad_startup)

def reference(unit_zone, up_window, down_window, switchable, capacity, fixed_cost, start_cost, fuel_cost, demand, commit, output, startup, price, link_dual, up_dual, down_dual):
    onehot = (unit_zone[None, :] == jnp.arange(Z, dtype=jnp.int32)[:, None]).astype(jnp.float32)
    floor_commit = (1 - switchable).astype(jnp.float32)[:, None]
    limit = capacity[:, None]
    weight = jnp.ones((), jnp.float32)
    for sweep in range(2):
        primal_step = step_scale / weight
        dual_step = step_scale * weight
        grad_commit, grad_startup = adjoint_terms(link_dual, up_dual, down_dual, up_window, down_window)
        grad_output = jnp.dot(onehot.T, price, precision=lax.Precision.HIGHEST)
        new_commit, new_output = project_pair(commit - primal_step * (fixed_cost[:, None] + grad_commit), output - primal_step * (fuel_cost + grad_output), floor_commit, limit)
        new_startup = jnp.clip(startup - primal_step * (start_cost[:, None] + grad_startup), 0.0, 1.0)
        reflect_commit = 2.0 * new_commit - commit
        reflect_output = 2.0 * new_output - output
        reflect_startup = 2.0 * new_startup - startup
        link, upper, lower = constraint_rows(reflect_commit, reflect_startup, up_window, down_window)
        balance = jnp.dot(onehot, reflect_output, precision=lax.Precision.HIGHEST)
        new_price = price + dual_step * (balance - demand)
        new_link = jnp.maximum(link_dual + dual_step * link, 0.0)
        new_up = jnp.maximum(up_dual + dual_step * upper, 0.0)
        new_down = jnp.maximum(down_dual + dual_step * lower, 0.0)
        if sweep == 0:
            primal_change = jnp.sum(jnp.square(new_commit - commit)) + jnp.sum(jnp.square(new_output - output)) + jnp.sum(jnp.square(new_startup - startup))
            dual_change = jnp.sum(jnp.square(new_price - price)) + jnp.sum(jnp.square(new_link - link_dual)) + jnp.sum(jnp.square(new_up - up_dual)) + jnp.sum(jnp.square(new_down - down_dual))
            weight = jnp.sqrt(jnp.sqrt((dual_change + epsilon) / (primal_change + epsilon)))
        commit, output, startup = (new_commit, new_output, new_startup)
        price, link_dual, up_dual, down_dual = (new_price, new_link, new_up, new_down)
    return (commit, output, startup, price, link_dual, up_dual, down_dual)
```

```python
import functools

import jax
import jax.numpy as jnp
from jax import lax
from jax.experimental import pallas as pl
from jax.experimental.pallas import tpu as pltpu
from jax.sharding import PartitionSpec as P

WIN = 24
BITS = 5
LANES = 128
ROW = 8
FIRST = ROW + 2 * WIN

step_scale = 0.015
epsilon = 1e-06

MESH = pl.DeviceIdType.MESH


def later(x, k):
    return pltpu.roll(x, k, 0)


def sooner(x, k):
    return pltpu.roll(x, x.shape[0] - k, 0)


def bits_of(window, shape):
    wide = jnp.broadcast_to(window, shape)
    return [(wide & (1 << b)) != 0 for b in range(BITS)]


def doubled(x, move):
    sums = [x]
    for b in range(BITS - 1):
        sums.append(sums[-1] + move(sums[-1], 1 << b))
    return sums


def windowed(sums, bits, move, beyond=None):
    if beyond is None:
        total = jnp.where(bits[0], sums[0], 0.0)
    else:
        total = jnp.where(bits[0], sums[0] + move(beyond, 1), beyond)
    for b in range(1, BITS):
        total = jnp.where(bits[b], sums[b] + move(total, 1 << b), total)
    return total


def tile_sum(x):
    return jnp.sum(x.reshape(-1, ROW, x.shape[1]), axis=0)


def split_dot(a, b, dims, split_first):
    whole = a if split_first else b
    high = whole.astype(jnp.bfloat16)
    low = (whole - high.astype(jnp.float32)).astype(jnp.bfloat16)
    total = None
    for part in (high, low):
        pair = (part, b) if split_first else (a, part)
        term = lax.dot_general(*pair, (dims, ((), ())), preferred_element_type=jnp.float32)
        total = term if total is None else total + term
    return total


def kernel(
    n_hours,
    n_units,
    unit_zone,
    up_window,
    down_window,
    switchable,
    capacity,
    fixed_cost,
    start_cost,
    fuel_hbm,
    demand_hbm,
    commit_hbm,
    output_hbm,
    startup_hbm,
    price_hbm,
    link_hbm,
    up_hbm,
    down_hbm,
    commit_res,
    output_res,
    startup_res,
    price_res,
    link_res,
    up_res,
    down_res,
    inbuf,
    outbuf,
    price_v,
    demand_v,
    ipar,
    fpar,
    state,
    reflect,
    grads,
    send_first,
    halo_first,
    send_last,
    halo_last,
    partial,
    others,
    change,
    slots,
    in_sem,
    small_sem,
    out_sem,
    price_sem,
    sf_sem,
    rf_sem,
    sl_sem,
    rl_sem,
    sp_sem,
    rp_sem,
    sw_sem,
    rw_sem,
):
    hour = lax.axis_index("hours")
    unit = lax.axis_index("units")
    me = hour * n_units + unit
    n_all = n_hours * n_units
    following = lax.rem(hour + 1, n_hours)
    preceding = lax.rem(hour + n_hours - 1, n_hours)
    chunks = state.shape[1]
    span = state.shape[2]
    zones = price_v.shape[0]
    C, G, S, F, B, M, N = range(7)

    sources = (commit_hbm, output_hbm, startup_hbm, fuel_hbm, link_hbm, up_hbm, down_hbm)
    loads = [pltpu.make_async_copy(src, inbuf.at[i], in_sem.at[i]) for i, src in enumerate(sources)]
    price_load = pltpu.make_async_copy(price_hbm, price_v, small_sem.at[0])
    demand_load = pltpu.make_async_copy(demand_hbm, demand_v, small_sem.at[1])
    for i in (B, M, N, C, S, G, F):
        loads[i].start()
    price_load.start()
    demand_load.start()

    barrier = pltpu.get_barrier_semaphore()

    def greet(k, carry):
        peer = lax.rem(me + k, n_all)
        pl.semaphore_signal(
            barrier,
            inc=1,
            device_id={"hours": peer // n_units, "units": lax.rem(peer, n_units)},
            device_id_type=MESH,
        )
        return carry

    lax.fori_loop(1, n_all, greet, 0)

    for c in range(chunks):
        part = pl.ds(c * LANES, LANES)
        ipar[c, 0:1, :] = up_window[part].reshape(1, LANES)
        ipar[c, 1:2, :] = down_window[part].reshape(1, LANES)
        ipar[c, 2:3, :] = unit_zone[part].reshape(1, LANES)
        limit = capacity[part].reshape(1, LANES)
        fpar[c, 0:1, :] = limit
        fpar[c, 1:2, :] = 1.0 / (1.0 + limit * limit)
        fpar[c, 2:3, :] = jnp.where(switchable[part].reshape(1, LANES) == 0, 2.0, -3e38)
        fpar[c, 3:4, :] = fixed_cost[part].reshape(1, LANES)
        fpar[c, 4:5, :] = start_cost[part].reshape(1, LANES)

    def rows_of(c):
        return pl.ds(pl.multiple_of(c * LANES, LANES), LANES)

    def first_copy(sweep, c):
        return pltpu.make_async_remote_copy(
            src_ref=send_first.at[sweep, c],
            dst_ref=halo_first.at[sweep, c],
            send_sem=sf_sem.at[sweep, c],
            recv_sem=rf_sem.at[sweep, c],
            device_id={"hours": preceding},
            device_id_type=MESH,
        )

    def last_copy(sweep, c):
        return pltpu.make_async_remote_copy(
            src_ref=send_last.at[sweep, c],
            dst_ref=halo_last.at[sweep, c],
            send_sem=sl_sem.at[sweep, c],
            recv_sem=rl_sem.at[sweep, c],
            device_id={"hours": following},
            device_id_type=MESH,
        )

    def partial_copy(sweep, k):
        return pltpu.make_async_remote_copy(
            src_ref=partial.at[sweep],
            dst_ref=others.at[sweep, k - 1],
            send_sem=sp_sem.at[sweep, k - 1],
            recv_sem=rp_sem.at[sweep, k - 1],
            device_id={"units": lax.rem(unit + k, n_units)},
            device_id_type=MESH,
        )

    def put_first(sweep, c, link, up, down):
        send_first[sweep, c, 0:ROW, :] = link[0:ROW]
        send_first[sweep, c, ROW : ROW + WIN, :] = up[0:WIN]
        send_first[sweep, c, ROW + WIN : FIRST, :] = down[0:WIN]

    for i in (B, M, N):
        loads[i].wait()

    def turn_duals(c, carry):
        link, up, down = (inbuf[i, rows_of(c), :].T for i in (B, M, N))
        state[B, c] = link
        state[M, c] = up
        state[N, c] = down
        put_first(0, c, link, up, down)
        return carry

    lax.fori_loop(0, chunks, turn_duals, 0)
    pl.semaphore_wait(barrier, n_all - 1)

    def send_duals(c, carry):
        first_copy(0, c).start()
        return carry

    lax.fori_loop(0, chunks, send_duals, 0)
    for i in (C, S, G, F):
        loads[i].wait()

    def turn_rest(c, carry):
        for i in (C, G, S, F):
            state[i, c] = inbuf[i, rows_of(c), :].T
        return carry

    lax.fori_loop(0, chunks, turn_rest, 0)
    price_load.wait()
    demand_load.wait()
    change[...] = jnp.zeros_like(change)

    def onehot_of(c):
        rank = lax.broadcasted_iota(jnp.int32, (zones, LANES), 0)
        hit = rank == jnp.broadcast_to(ipar[c, 2:3, :], (zones, LANES))
        return jnp.where(hit, 1.0, 0.0).astype(jnp.bfloat16)

    def adjoint(sweep, c, carry):
        first_copy(sweep, c).wait_recv()
        link, up, down = (state[i, c] for i in (B, M, N))
        rim = halo_first.at[sweep, c]
        long = (span + WIN, LANES)
        up_bits = bits_of(ipar[c, 0:1, :], long)
        down_bits = bits_of(ipar[c, 1:2, :], long)
        up_long = jnp.concatenate([up, rim[ROW : ROW + WIN, :]], axis=0)
        total = windowed(doubled(up_long, sooner), up_bits, sooner)[:span] - link
        down_long = jnp.concatenate([down, rim[ROW + WIN : FIRST, :]], axis=0)
        total = total + windowed(doubled(down_long, sooner), down_bits, sooner)[:span]
        grads[1, c] = total
        lagged = down_long
        for b in range(BITS):
            lagged = jnp.where(down_bits[b], sooner(lagged, 1 << b), lagged)
        link_long = jnp.concatenate([link, rim[0:ROW, :]], axis=0)
        grads[0, c] = link - sooner(link_long, 1)[:span] - up + lagged[:span]
        return carry

    def primal(sweep, step, c, carry):
        limit = fpar[c, 0:1, :]
        onehot = onehot_of(c)
        commit, output, startup = (state[i, c] for i in (C, G, S))
        grad_output = split_dot(price_v[...], onehot, ((0,), (0,)), True)
        point_x = commit - step * (fpar[c, 3:4, :] + grads[0, c])
        point_g = output - step * (state[F, c] + grad_output)
        point_x = jnp.maximum(point_x, fpar[c, 2:3, :])
        above = point_g > limit * point_x
        ratio = jnp.clip((point_x + limit * point_g) * fpar[c, 1:2, :], 0.0, 1.0)
        new_commit = jnp.where(above, ratio, jnp.clip(point_x, 0.0, 1.0))
        new_output = jnp.where(above, limit * ratio, jnp.minimum(jnp.maximum(point_g, 0.0), limit))
        new_startup = jnp.clip(startup - step * (fpar[c, 4:5, :] + grads[1, c]), 0.0, 1.0)
        reflect_commit = 2.0 * new_commit - commit
        reflect_startup = 2.0 * new_startup - startup
        reflect[0, c] = reflect_commit
        reflect[1, c] = reflect_startup
        send_last[sweep, c, 0:WIN, :] = reflect_commit[span - WIN :]
        send_last[sweep, c, WIN:, :] = reflect_startup[span - WIN :]
        last_copy(sweep, c).start()
        reflect_output = 2.0 * new_output - output
        partial[sweep] += split_dot(onehot, reflect_output, ((1,), (1,)), False)
        if sweep == 0:
            change[0:ROW, :] += (
                tile_sum(jnp.square(new_commit - commit))
                + tile_sum(jnp.square(new_output - output))
                + tile_sum(jnp.square(new_startup - startup))
            )
            state[C, c] = new_commit
            state[G, c] = new_output
            state[S, c] = new_startup
        else:
            give(0, c, new_commit)
            give(1, c, new_output)
            give(2, c, new_startup)
        return carry

    results = (commit_res, output_res, startup_res, link_res, up_res, down_res)

    def store_of(i, c):
        return pltpu.make_async_copy(
            outbuf.at[i, rows_of(c), :], results[i].at[rows_of(c), :], out_sem.at[i, c]
        )

    def give(i, c, value):
        outbuf[i, rows_of(c), :] = value.T
        store_of(i, c).start()

    def rows(sweep, step, c, carry):
        last_copy(sweep, c).wait_recv()
        rim = halo_last.at[sweep, c]
        commit, startup = reflect[0, c], reflect[1, c]
        commit_long = jnp.concatenate([rim[0:WIN, :], commit], axis=0)
        startup_long = jnp.concatenate([rim[WIN:, :], startup], axis=0)
        long = (span + WIN, LANES)
        up_bits = bits_of(ipar[c, 0:1, :], long)
        down_bits = bits_of(ipar[c, 1:2, :], long)
        sums = doubled(startup_long, later)
        upper = windowed(sums, up_bits, later)[WIN:] - commit
        lower = windowed(sums, down_bits, later, commit_long)[WIN:] - 1.0
        link = commit - later(commit_long, 1)[WIN:] - startup
        olds = tuple(state[i, c] for i in (B, M, N))
        news = tuple(
            jnp.maximum(old + step * row, 0.0) for old, row in zip(olds, (link, upper, lower))
        )
        if sweep == 0:
            put_first(1, c, *news)
            first_copy(1, c).start()
            squares = [tile_sum(jnp.square(new - old)) for new, old in zip(news, olds)]
            change[ROW:, :] += squares[0] + squares[1] + squares[2]
            for i, new in zip((B, M, N), news):
                state[i, c] = new
        else:
            for i, new in enumerate(news):
                give(3 + i, c, new)
        return carry

    def totals(sweep):
        total = partial[sweep]
        for k in range(1, n_units):
            partial_copy(sweep, k).wait_recv()
            total = total + others[sweep, k - 1]
        return total

    def weight_copy(k):
        peer = lax.rem(me + k, n_all)
        return pltpu.make_async_remote_copy(
            src_ref=slots.at[me],
            dst_ref=slots.at[me],
            send_sem=sw_sem.at[k],
            recv_sem=rw_sem.at[me],
            device_id={"hours": peer // n_units, "units": lax.rem(peer, n_units)},
            device_id_type=MESH,
        )

    def weight_arrival(k):
        peer = lax.rem(me + k, n_all)
        return pltpu.make_async_remote_copy(
            src_ref=slots.at[peer],
            dst_ref=slots.at[peer],
            send_sem=sw_sem.at[k],
            recv_sem=rw_sem.at[peer],
            device_id={"hours": peer // n_units, "units": lax.rem(peer, n_units)},
            device_id_type=MESH,
        )

    primal_step = step_scale
    dual_step = step_scale
    for sweep in range(2):
        partial[sweep] = jnp.zeros((zones, span), jnp.float32)
        if sweep == 0:

            def both(c, carry):
                adjoint(0, c, 0)
                return primal(0, step_scale, c, carry)

            lax.fori_loop(0, chunks, both, 0)
        else:
            lax.fori_loop(0, chunks, functools.partial(adjoint, 1), 0)

            def send_done(k, carry):
                weight_arrival(k).wait_recv()
                return carry

            lax.fori_loop(1, n_all, send_done, 0)
            summed = jnp.sum(slots[...], axis=0)
            primal_change = jnp.sum(summed[:ROW], keepdims=True)
            dual_change = jnp.sum(summed[ROW:], keepdims=True)
            weight = jnp.sqrt(jnp.sqrt((dual_change + epsilon) / (primal_change + epsilon)))
            primal_step = jnp.broadcast_to(step_scale / weight, (1, LANES))
            dual_step = jnp.broadcast_to(step_scale * weight, (1, LANES))
            lax.fori_loop(0, chunks, functools.partial(primal, 1, primal_step), 0)
        for k in range(1, n_units):
            partial_copy(sweep, k).start()
        lax.fori_loop(0, chunks, functools.partial(rows, sweep, dual_step), 0)
        price = price_v[...]
        new_price = price + dual_step * (totals(sweep) - demand_v[...])
        price_v[...] = new_price
        if sweep == 0:
            change[ROW:, :] += tile_sum(jnp.square(new_price - price)) * (1.0 / n_units)
            slots[me] = change[...]

            def send_weight(k, carry):
                weight_copy(k).start()
                return carry

            lax.fori_loop(1, n_all, send_weight, 0)

    price_store = pltpu.make_async_copy(price_v, price_res, price_sem)
    price_store.start()

    def finish(c, carry):
        for sweep in range(2):
            first_copy(sweep, c).wait_send()
            last_copy(sweep, c).wait_send()
        for i in range(6):
            store_of(i, c).wait()
        return carry

    lax.fori_loop(0, chunks, finish, 0)
    for sweep in range(2):
        for k in range(1, n_units):
            partial_copy(sweep, k).wait_send()

    def finish_weight(k, carry):
        weight_copy(k).wait_send()
        return carry

    lax.fori_loop(1, n_all, finish_weight, 0)
    price_store.wait()


def body(*args):
    n_hours = lax.axis_size("hours")
    n_units = lax.axis_size("units")
    n_all = n_hours * n_units
    fuel_cost, demand = args[7], args[8]
    units, span = fuel_cost.shape
    zones = demand.shape[0]
    chunks = units // LANES
    f32 = jnp.float32
    wide = jax.ShapeDtypeStruct((units, span), f32)
    small = jax.ShapeDtypeStruct((zones, span), f32)
    vmem = pl.BlockSpec(memory_space=pltpu.VMEM)
    anywhere = pl.BlockSpec(memory_space=pl.ANY)
    dma = pltpu.SemaphoreType.DMA
    peers = max(n_units - 1, 1)
    return pl.pallas_call(
        functools.partial(kernel, n_hours, n_units),
        out_shape=(wide, wide, wide, small, wide, wide, wide),
        in_specs=[vmem] * 7 + [anywhere] * 9,
        out_specs=[anywhere] * 7,
        scratch_shapes=[
            pltpu.VMEM((7, units, span), f32),
            pltpu.VMEM((6, units, span), f32),
            pltpu.VMEM((zones, span), f32),
            pltpu.VMEM((zones, span), f32),
            pltpu.VMEM((chunks, ROW, LANES), jnp.int32),
            pltpu.VMEM((chunks, ROW, LANES), f32),
            pltpu.VMEM((7, chunks, span, LANES), f32),
            pltpu.VMEM((2, chunks, span, LANES), f32),
            pltpu.VMEM((2, chunks, span, LANES), f32),
            pltpu.VMEM((2, chunks, FIRST, LANES), f32),
            pltpu.VMEM((2, chunks, FIRST, LANES), f32),
            pltpu.VMEM((2, chunks, 2 * WIN, LANES), f32),
            pltpu.VMEM((2, chunks, 2 * WIN, LANES), f32),
            pltpu.VMEM((2, zones, span), f32),
            pltpu.VMEM((2, peers, zones, span), f32),
            pltpu.VMEM((2 * ROW, LANES), f32),
            pltpu.VMEM((n_all, 2 * ROW, LANES), f32),
            dma((7,)),
            dma((2,)),
            dma((6, chunks)),
            dma,
            dma((2, chunks)),
            dma((2, chunks)),
            dma((2, chunks)),
            dma((2, chunks)),
            dma((2, peers)),
            dma((2, peers)),
            dma((n_all,)),
            dma((n_all,)),
        ],
        compiler_params=pltpu.CompilerParams(
            collective_id=0, has_side_effects=True, vmem_limit_bytes=24 * 1024 * 1024
        ),
    )(*args)


def solution(mesh):
    unit = P("units")
    wide = P(("groups", "units"), "hours")
    zonal = P("groups", "hours")
    return jax.shard_map(
        body,
        mesh=mesh,
        in_specs=(unit,) * 7 + (wide, zonal, wide, wide, wide, zonal, wide, wide, wide),
        out_specs=(wide, wide, wide, zonal, wide, wide, wide),
        check_vma=False,
    )
```

```python
import functools

import jax
import jax.numpy as jnp
from jax import lax
from jax.experimental import pallas as pl
from jax.experimental.pallas import tpu as pltpu
from jax.sharding import PartitionSpec as P

WIN = 24
BITS = 5
LANES = 128
ROW = 8
FIRST = ROW + 2 * WIN

step_scale = 0.015
epsilon = 1e-06

MESH = pl.DeviceIdType.MESH


def later(x, k):
    return pltpu.roll(x, k, 0)


def sooner(x, k):
    return pltpu.roll(x, x.shape[0] - k, 0)


def bits_of(window, shape):
    wide = jnp.broadcast_to(window, shape)
    return [(wide & (1 << b)) != 0 for b in range(BITS)]


def doubled(x, move):
    sums = [x]
    for b in range(BITS - 1):
        sums.append(sums[-1] + move(sums[-1], 1 << b))
    return sums


def windowed(sums, bits, move, beyond=None):
    if beyond is None:
        total = jnp.where(bits[0], sums[0], 0.0)
    else:
        total = jnp.where(bits[0], sums[0] + move(beyond, 1), beyond)
    for b in range(1, BITS):
        total = jnp.where(bits[b], sums[b] + move(total, 1 << b), total)
    return total


def tile_sum(x):
    return jnp.sum(x.reshape(-1, ROW, x.shape[1]), axis=0)


def zone_sums(onehot, values):
    high = values.astype(jnp.bfloat16)
    low = (values - high.astype(jnp.float32)).astype(jnp.bfloat16)
    return lax.dot_general(
        jnp.concatenate([onehot, onehot], axis=1),
        jnp.concatenate([high, low], axis=1),
        (((1,), (1,)), ((), ())),
        preferred_element_type=jnp.float32,
    )


def kernel(
    n_hours,
    n_units,
    unit_zone_hbm,
    up_window_hbm,
    down_window_hbm,
    switchable_hbm,
    capacity_hbm,
    fixed_cost_hbm,
    start_cost_hbm,
    fuel_hbm,
    demand_hbm,
    commit_hbm,
    output_hbm,
    startup_hbm,
    price_hbm,
    link_hbm,
    up_hbm,
    down_hbm,
    turned_hbm,
    price_res,
    unit_zone,
    up_window,
    down_window,
    switchable,
    capacity,
    fixed_cost,
    start_cost,
    inbuf,
    turned,
    price_v,
    price_parts,
    onehots,
    demand_v,
    ipar,
    fpar,
    state,
    reflect,
    grads,
    send_first,
    halo_first,
    send_last,
    halo_last,
    partial,
    others,
    change,
    slots,
    in_sem,
    small_sem,
    unit_sem,
    out_sem,
    price_sem,
    sf_sem,
    rf_sem,
    sl_sem,
    rl_sem,
    sp_sem,
    rp_sem,
    sw_sem,
    rw_sem,
):
    hour = lax.axis_index("hours")
    unit = lax.axis_index("units")
    me = hour * n_units + unit
    n_all = n_hours * n_units
    following = lax.rem(hour + 1, n_hours)
    preceding = lax.rem(hour + n_hours - 1, n_hours)
    chunks = state.shape[1]
    span = state.shape[2]
    zones = price_v.shape[0]
    C, G, S, F, B, M, N = range(7)

    sources = (commit_hbm, output_hbm, startup_hbm, fuel_hbm, link_hbm, up_hbm, down_hbm)
    loads = [pltpu.make_async_copy(src, inbuf.at[i], in_sem.at[i]) for i, src in enumerate(sources)]
    price_load = pltpu.make_async_copy(price_hbm, price_v, small_sem.at[0])
    demand_load = pltpu.make_async_copy(demand_hbm, demand_v, small_sem.at[1])
    unit_pairs = (
        (unit_zone_hbm, unit_zone),
        (up_window_hbm, up_window),
        (down_window_hbm, down_window),
        (switchable_hbm, switchable),
        (capacity_hbm, capacity),
        (fixed_cost_hbm, fixed_cost),
        (start_cost_hbm, start_cost),
    )
    unit_loads = [
        pltpu.make_async_copy(src, dst, unit_sem.at[i]) for i, (src, dst) in enumerate(unit_pairs)
    ]
    for i in (B, M, N):
        loads[i].start()
    for load in unit_loads:
        load.start()
    for i in (C, S, G, F):
        loads[i].start()
    price_load.start()
    demand_load.start()

    barrier = pltpu.get_barrier_semaphore()

    def greet(k, carry):
        peer = lax.rem(me + k, n_all)
        pl.semaphore_signal(
            barrier,
            inc=1,
            device_id={"hours": peer // n_units, "units": lax.rem(peer, n_units)},
            device_id_type=MESH,
        )
        return carry

    lax.fori_loop(1, n_all, greet, 0)

    def rows_of(c):
        return pl.ds(pl.multiple_of(c * LANES, LANES), LANES)

    def first_copy(sweep, c):
        return pltpu.make_async_remote_copy(
            src_ref=send_first.at[sweep, c],
            dst_ref=halo_first.at[sweep, c],
            send_sem=sf_sem.at[sweep, c],
            recv_sem=rf_sem.at[sweep, c],
            device_id={"hours": preceding},
            device_id_type=MESH,
        )

    def last_copy(sweep, c):
        return pltpu.make_async_remote_copy(
            src_ref=send_last.at[sweep, c],
            dst_ref=halo_last.at[sweep, c],
            send_sem=sl_sem.at[sweep, c],
            recv_sem=rl_sem.at[sweep, c],
            device_id={"hours": following},
            device_id_type=MESH,
        )

    def partial_copy(sweep, k):
        return pltpu.make_async_remote_copy(
            src_ref=partial.at[sweep],
            dst_ref=others.at[sweep, k - 1],
            send_sem=sp_sem.at[sweep, k - 1],
            recv_sem=rp_sem.at[sweep, k - 1],
            device_id={"units": lax.rem(unit + k, n_units)},
            device_id_type=MESH,
        )

    def put_first(sweep, c, link, up, down):
        send_first[sweep, c, 0:ROW, :] = link[0:ROW]
        send_first[sweep, c, ROW : ROW + WIN, :] = up[0:WIN]
        send_first[sweep, c, ROW + WIN : FIRST, :] = down[0:WIN]

    for i in (B, M, N):
        loads[i].wait()

    def turn_duals(c, carry):
        link, up, down = (inbuf[i, rows_of(c), :].T for i in (B, M, N))
        state[B, c] = link
        state[M, c] = up
        state[N, c] = down
        put_first(0, c, link, up, down)
        return carry

    lax.fori_loop(0, chunks, turn_duals, 0)
    pl.semaphore_wait(barrier, n_all - 1)

    def send_duals(c, carry):
        first_copy(0, c).start()
        return carry

    lax.fori_loop(0, chunks, send_duals, 0)
    for load in unit_loads:
        load.wait()
    for c in range(chunks):
        part = pl.ds(c * LANES, LANES)
        ipar[c, 0:1, :] = up_window[part].reshape(1, LANES)
        ipar[c, 1:2, :] = down_window[part].reshape(1, LANES)
        ipar[c, 2:3, :] = unit_zone[part].reshape(1, LANES)
        limit = capacity[part].reshape(1, LANES)
        fpar[c, 0:1, :] = limit
        fpar[c, 1:2, :] = 1.0 / (1.0 + limit * limit)
        fpar[c, 2:3, :] = jnp.where(switchable[part].reshape(1, LANES) == 0, 2.0, -3e38)
        fpar[c, 3:4, :] = fixed_cost[part].reshape(1, LANES)
        fpar[c, 4:5, :] = start_cost[part].reshape(1, LANES)
        rank = lax.broadcasted_iota(jnp.int32, (zones, LANES), 0)
        hit = rank == jnp.broadcast_to(ipar[c, 2:3, :], (zones, LANES))
        onehot = jnp.where(hit, 1.0, 0.0).astype(jnp.bfloat16)
        onehots[c, 0:zones, :] = onehot
        onehots[c, zones:, :] = onehot
    for i in (C, S, G, F):
        loads[i].wait()

    def turn_rest(c, carry):
        for i in (C, G, S, F):
            state[i, c] = inbuf[i, rows_of(c), :].T
        return carry

    lax.fori_loop(0, chunks, turn_rest, 0)
    price_load.wait()
    demand_load.wait()
    change[...] = jnp.zeros_like(change)

    def part_price():
        turned_price = price_v[...].T
        high = turned_price.astype(jnp.bfloat16)
        low = (turned_price - high.astype(jnp.float32)).astype(jnp.bfloat16)
        price_parts[...] = jnp.concatenate([high, low], axis=1)

    def adjoint(sweep, c, carry):
        first_copy(sweep, c).wait_recv()
        link, up, down = (state[i, c] for i in (B, M, N))
        rim = halo_first.at[sweep, c]
        long = (span + WIN, LANES)
        up_bits = bits_of(ipar[c, 0:1, :], long)
        down_bits = bits_of(ipar[c, 1:2, :], long)
        up_long = jnp.concatenate([up, rim[ROW : ROW + WIN, :]], axis=0)
        total = windowed(doubled(up_long, sooner), up_bits, sooner)[:span] - link
        down_long = jnp.concatenate([down, rim[ROW + WIN : FIRST, :]], axis=0)
        total = total + windowed(doubled(down_long, sooner), down_bits, sooner)[:span]
        grads[1, c] = total
        lagged = down_long
        for b in range(BITS):
            lagged = jnp.where(down_bits[b], sooner(lagged, 1 << b), lagged)
        link_long = jnp.concatenate([link, rim[0:ROW, :]], axis=0)
        grads[0, c] = link - sooner(link_long, 1)[:span] - up + lagged[:span]
        return carry

    def primal(sweep, step, c, carry):
        limit = fpar[c, 0:1, :]
        commit, output, startup = (state[i, c] for i in (C, G, S))
        grad_output = jnp.dot(price_parts[...], onehots[c], preferred_element_type=jnp.float32)
        point_x = commit - step * (fpar[c, 3:4, :] + grads[0, c])
        point_g = output - step * (state[F, c] + grad_output)
        point_x = jnp.maximum(point_x, fpar[c, 2:3, :])
        above = point_g > limit * point_x
        ratio = jnp.clip((point_x + limit * point_g) * fpar[c, 1:2, :], 0.0, 1.0)
        new_commit = jnp.where(above, ratio, jnp.clip(point_x, 0.0, 1.0))
        new_output = jnp.where(above, limit * ratio, jnp.minimum(jnp.maximum(point_g, 0.0), limit))
        new_startup = jnp.clip(startup - step * (fpar[c, 4:5, :] + grads[1, c]), 0.0, 1.0)
        reflect_commit = 2.0 * new_commit - commit
        reflect_startup = 2.0 * new_startup - startup
        reflect[0, c] = reflect_commit
        reflect[1, c] = reflect_startup
        send_last[sweep, c, 0:WIN, :] = reflect_commit[span - WIN :]
        send_last[sweep, c, WIN:, :] = reflect_startup[span - WIN :]
        last_copy(sweep, c).start()
        reflect_output = 2.0 * new_output - output
        partial[sweep] += zone_sums(onehots[c, 0:zones, :], reflect_output)
        if sweep == 0:
            change[0:ROW, :] += (
                tile_sum(jnp.square(new_commit - commit))
                + tile_sum(jnp.square(new_output - output))
                + tile_sum(jnp.square(new_startup - startup))
            )
            state[C, c] = new_commit
            state[G, c] = new_output
            state[S, c] = new_startup
        else:
            give(0, c, new_commit)
            give(1, c, new_output)
            give(2, c, new_startup)
        return carry

    def store_of(i, c):
        return pltpu.make_async_copy(turned.at[i, c], turned_hbm.at[i, c], out_sem.at[i, c])

    def give(i, c, value):
        turned[i, c] = value
        store_of(i, c).start()

    def rows(sweep, step, c, carry):
        last_copy(sweep, c).wait_recv()
        rim = halo_last.at[sweep, c]
        commit, startup = reflect[0, c], reflect[1, c]
        commit_long = jnp.concatenate([rim[0:WIN, :], commit], axis=0)
        startup_long = jnp.concatenate([rim[WIN:, :], startup], axis=0)
        long = (span + WIN, LANES)
        up_bits = bits_of(ipar[c, 0:1, :], long)
        down_bits = bits_of(ipar[c, 1:2, :], long)
        sums = doubled(startup_long, later)
        upper = windowed(sums, up_bits, later)[WIN:] - commit
        lower = windowed(sums, down_bits, later, commit_long)[WIN:] - 1.0
        link = commit - later(commit_long, 1)[WIN:] - startup
        olds = tuple(state[i, c] for i in (B, M, N))
        news = tuple(
            jnp.maximum(old + step * row, 0.0) for old, row in zip(olds, (link, upper, lower))
        )
        if sweep == 0:
            put_first(1, c, *news)
            first_copy(1, c).start()
            squares = [tile_sum(jnp.square(new - old)) for new, old in zip(news, olds)]
            change[ROW:, :] += squares[0] + squares[1] + squares[2]
            for i, new in zip((B, M, N), news):
                state[i, c] = new
        else:
            for i, new in enumerate(news):
                give(3 + i, c, new)
        return carry

    def totals(sweep):
        total = partial[sweep]
        for k in range(1, n_units):
            partial_copy(sweep, k).wait_recv()
            total = total + others[sweep, k - 1]
        return total

    def weight_copy(k):
        peer = lax.rem(me + k, n_all)
        return pltpu.make_async_remote_copy(
            src_ref=slots.at[me],
            dst_ref=slots.at[me],
            send_sem=sw_sem.at[k],
            recv_sem=rw_sem.at[me],
            device_id={"hours": peer // n_units, "units": lax.rem(peer, n_units)},
            device_id_type=MESH,
        )

    def weight_arrival(k):
        peer = lax.rem(me + k, n_all)
        return pltpu.make_async_remote_copy(
            src_ref=slots.at[peer],
            dst_ref=slots.at[peer],
            send_sem=sw_sem.at[k],
            recv_sem=rw_sem.at[peer],
            device_id={"hours": peer // n_units, "units": lax.rem(peer, n_units)},
            device_id_type=MESH,
        )

    primal_step = step_scale
    dual_step = step_scale
    for sweep in range(2):
        partial[sweep] = jnp.zeros((zones, span), jnp.float32)
        part_price()
        if sweep == 0:

            def both(c, carry):
                adjoint(0, c, 0)
                return primal(0, step_scale, c, carry)

            lax.fori_loop(0, chunks, both, 0)
        else:
            lax.fori_loop(0, chunks, functools.partial(adjoint, 1), 0)

            def send_done(k, carry):
                weight_arrival(k).wait_recv()
                return carry

            lax.fori_loop(1, n_all, send_done, 0)
            summed = jnp.sum(slots[...], axis=0)
            primal_change = jnp.sum(summed[:ROW], keepdims=True)
            dual_change = jnp.sum(summed[ROW:], keepdims=True)
            weight = jnp.sqrt(jnp.sqrt((dual_change + epsilon) / (primal_change + epsilon)))
            primal_step = jnp.broadcast_to(step_scale / weight, (1, LANES))
            dual_step = jnp.broadcast_to(step_scale * weight, (1, LANES))
            lax.fori_loop(0, chunks, functools.partial(primal, 1, primal_step), 0)
        for k in range(1, n_units):
            partial_copy(sweep, k).start()
        lax.fori_loop(0, chunks, functools.partial(rows, sweep, dual_step), 0)
        price = price_v[...]
        new_price = price + dual_step * (totals(sweep) - demand_v[...])
        price_v[...] = new_price
        if sweep == 0:
            change[ROW:, :] += tile_sum(jnp.square(new_price - price)) * (1.0 / n_units)
            slots[me] = change[...]

            def send_weight(k, carry):
                weight_copy(k).start()
                return carry

            lax.fori_loop(1, n_all, send_weight, 0)


    price_store = pltpu.make_async_copy(price_v, price_res, price_sem)
    price_store.start()

    def finish(c, carry):
        for sweep in range(2):
            first_copy(sweep, c).wait_send()
            last_copy(sweep, c).wait_send()
        for i in range(6):
            store_of(i, c).wait()
        return carry

    lax.fori_loop(0, chunks, finish, 0)
    for sweep in range(2):
        for k in range(1, n_units):
            partial_copy(sweep, k).wait_send()

    def finish_weight(k, carry):
        weight_copy(k).wait_send()
        return carry

    lax.fori_loop(1, n_all, finish_weight, 0)
    price_store.wait()


def place(turned, price, *rest):
    results, price_res, held, outbuf, load_sem, sem, price_sem = rest[:6], *rest[6:]
    chunks = turned.shape[1]
    loads = [pltpu.make_async_copy(turned.at[i], held.at[i], load_sem.at[i]) for i in range(6)]
    stores = [pltpu.make_async_copy(outbuf.at[i], results[i], sem.at[i]) for i in range(6)]
    for load in loads:
        load.start()
    price_store = pltpu.make_async_copy(price, price_res, price_sem)
    price_store.start()
    for i in range(6):
        loads[i].wait()
        for c in range(chunks):
            outbuf[i, c * LANES : (c + 1) * LANES, :] = held[i, c].T
        stores[i].start()
    for store in stores:
        store.wait()
    price_store.wait()


def body(*args):
    n_hours = lax.axis_size("hours")
    n_units = lax.axis_size("units")
    n_all = n_hours * n_units
    fuel_cost, demand = args[7], args[8]
    units, span = fuel_cost.shape
    zones = demand.shape[0]
    chunks = units // LANES
    f32 = jnp.float32
    wide = jax.ShapeDtypeStruct((units, span), f32)
    small = jax.ShapeDtypeStruct((zones, span), f32)
    hbm = pl.BlockSpec(memory_space=pltpu.HBM)
    dma = pltpu.SemaphoreType.DMA
    peers = max(n_units - 1, 1)
    turned, price = pl.pallas_call(
        functools.partial(kernel, n_hours, n_units),
        out_shape=(jax.ShapeDtypeStruct((6, chunks, span, LANES), f32), small),
        in_specs=[hbm] * 16,
        out_specs=[hbm] * 2,
        scratch_shapes=[
            *[pltpu.VMEM((units,), arg.dtype) for arg in args[:7]],
            pltpu.VMEM((7, units, span), f32),
            pltpu.VMEM((6, chunks, span, LANES), f32),
            pltpu.VMEM((zones, span), f32),
            pltpu.VMEM((span, 2 * zones), jnp.bfloat16),
            pltpu.VMEM((chunks, 2 * zones, LANES), jnp.bfloat16),
            pltpu.VMEM((zones, span), f32),
            pltpu.VMEM((chunks, ROW, LANES), jnp.int32),
            pltpu.VMEM((chunks, ROW, LANES), f32),
            pltpu.VMEM((7, chunks, span, LANES), f32),
            pltpu.VMEM((2, chunks, span, LANES), f32),
            pltpu.VMEM((2, chunks, span, LANES), f32),
            pltpu.VMEM((2, chunks, FIRST, LANES), f32),
            pltpu.VMEM((2, chunks, FIRST, LANES), f32),
            pltpu.VMEM((2, chunks, 2 * WIN, LANES), f32),
            pltpu.VMEM((2, chunks, 2 * WIN, LANES), f32),
            pltpu.VMEM((2, zones, span), f32),
            pltpu.VMEM((2, peers, zones, span), f32),
            pltpu.VMEM((2 * ROW, LANES), f32),
            pltpu.VMEM((n_all, 2 * ROW, LANES), f32),
            dma((7,)),
            dma((2,)),
            dma((7,)),
            dma((6, chunks)),
            dma,
            dma((2, chunks)),
            dma((2, chunks)),
            dma((2, chunks)),
            dma((2, chunks)),
            dma((2, peers)),
            dma((2, peers)),
            dma((n_all,)),
            dma((n_all,)),
        ],
        compiler_params=pltpu.CompilerParams(
            collective_id=0, has_side_effects=True, vmem_limit_bytes=56 * 1024 * 1024
        ),
    )(*args)
    commit, output, startup, link, up, down, price = pl.pallas_call(
        place,
        out_shape=(wide,) * 6 + (small,),
        in_specs=[hbm] * 2,
        out_specs=[hbm] * 7,
        scratch_shapes=[
            pltpu.VMEM((6, chunks, span, LANES), f32),
            pltpu.VMEM((6, units, span), f32),
            dma((6,)),
            dma((6,)),
            dma,
        ],
        compiler_params=pltpu.CompilerParams(vmem_limit_bytes=56 * 1024 * 1024),
    )(turned, price)
    return (commit, output, startup, price, link, up, down)


def solution(mesh):
    unit = P("units")
    wide = P(("groups", "units"), "hours")
    zonal = P("groups", "hours")
    return jax.shard_map(
        body,
        mesh=mesh,
        in_specs=(unit,) * 7 + (wide, zonal, wide, wide, wide, zonal, wide, wide, wide),
        out_specs=(wide, wide, wide, zonal, wide, wide, wide),
        check_vma=False,
    )
```

```python
import functools

import jax
import jax.numpy as jnp
from jax import lax
from jax.experimental import pallas as pl
from jax.experimental.pallas import tpu as pltpu
from jax.sharding import PartitionSpec as P

WIN = 24
BITS = 5
LANES = 128
ROW = 8
FIRST = ROW + 2 * WIN

step_scale = 0.015
epsilon = 1e-06

MESH = pl.DeviceIdType.MESH


def later(x, k):
    return pltpu.roll(x, k, 0)


def sooner(x, k):
    return pltpu.roll(x, x.shape[0] - k, 0)


def bits_of(window, shape):
    wide = jnp.broadcast_to(window, shape)
    return [(wide & (1 << b)) != 0 for b in range(BITS)]


def doubled(x, move):
    sums = [x]
    for b in range(BITS - 1):
        sums.append(sums[-1] + move(sums[-1], 1 << b))
    return sums


def windowed(sums, bits, move, beyond=None):
    if beyond is None:
        total = jnp.where(bits[0], sums[0], 0.0)
    else:
        total = jnp.where(bits[0], sums[0] + move(beyond, 1), beyond)
    for b in range(1, BITS):
        total = jnp.where(bits[b], sums[b] + move(total, 1 << b), total)
    return total


def tile_sum(x):
    return jnp.sum(x.reshape(-1, ROW, x.shape[1]), axis=0)


def two_parts(values):
    high = values.astype(jnp.bfloat16)
    low = (values - high.astype(jnp.float32)).astype(jnp.bfloat16)
    return jnp.concatenate([high, low], axis=1)


def kernel(
    n_hours,
    n_units,
    unit_zone_hbm,
    up_window_hbm,
    down_window_hbm,
    switchable_hbm,
    capacity_hbm,
    fixed_cost_hbm,
    start_cost_hbm,
    fuel_hbm,
    demand_hbm,
    commit_hbm,
    output_hbm,
    startup_hbm,
    price_hbm,
    link_hbm,
    up_hbm,
    down_hbm,
    turned_hbm,
    price_res,
    unit_zone,
    up_window,
    down_window,
    switchable,
    capacity,
    fixed_cost,
    start_cost,
    inbuf,
    turned,
    price_v,
    price_parts,
    onehots,
    spread,
    output_parts,
    demand_v,
    ipar,
    fpar,
    state,
    reflect,
    grads,
    send_first,
    halo_first,
    send_last,
    halo_last,
    partial,
    others,
    change,
    slots,
    in_sem,
    small_sem,
    unit_sem,
    out_sem,
    price_sem,
    sf_sem,
    rf_sem,
    sl_sem,
    rl_sem,
    sp_sem,
    rp_sem,
    sw_sem,
    rw_sem,
):
    hour = lax.axis_index("hours")
    unit = lax.axis_index("units")
    me = hour * n_units + unit
    n_all = n_hours * n_units
    following = lax.rem(hour + 1, n_hours)
    preceding = lax.rem(hour + n_hours - 1, n_hours)
    chunks = state.shape[1]
    span = state.shape[2]
    zones = price_v.shape[0]
    C, G, S, F, B, M, N = range(7)

    sources = (commit_hbm, output_hbm, startup_hbm, fuel_hbm, link_hbm, up_hbm, down_hbm)
    loads = [pltpu.make_async_copy(src, inbuf.at[i], in_sem.at[i]) for i, src in enumerate(sources)]
    price_load = pltpu.make_async_copy(price_hbm, price_v, small_sem.at[0])
    demand_load = pltpu.make_async_copy(demand_hbm, demand_v, small_sem.at[1])
    unit_pairs = (
        (unit_zone_hbm, unit_zone),
        (up_window_hbm, up_window),
        (down_window_hbm, down_window),
        (switchable_hbm, switchable),
        (capacity_hbm, capacity),
        (fixed_cost_hbm, fixed_cost),
        (start_cost_hbm, start_cost),
    )
    unit_loads = [
        pltpu.make_async_copy(src, dst, unit_sem.at[i]) for i, (src, dst) in enumerate(unit_pairs)
    ]
    for i in (B, M, N):
        loads[i].start()
    for load in unit_loads:
        load.start()
    for i in (C, S, G, F):
        loads[i].start()
    price_load.start()
    demand_load.start()

    barrier = pltpu.get_barrier_semaphore()

    def greet(k, carry):
        peer = lax.rem(me + k, n_all)
        pl.semaphore_signal(
            barrier,
            inc=1,
            device_id={"hours": peer // n_units, "units": lax.rem(peer, n_units)},
            device_id_type=MESH,
        )
        return carry

    lax.fori_loop(1, n_all, greet, 0)

    def rows_of(c):
        return pl.ds(c * LANES, LANES)

    def first_copy(sweep, c):
        return pltpu.make_async_remote_copy(
            src_ref=send_first.at[sweep, c],
            dst_ref=halo_first.at[sweep, c],
            send_sem=sf_sem.at[sweep, c],
            recv_sem=rf_sem.at[sweep, c],
            device_id={"hours": preceding},
            device_id_type=MESH,
        )

    def last_copy(sweep, c):
        return pltpu.make_async_remote_copy(
            src_ref=send_last.at[sweep, c],
            dst_ref=halo_last.at[sweep, c],
            send_sem=sl_sem.at[sweep, c],
            recv_sem=rl_sem.at[sweep, c],
            device_id={"hours": following},
            device_id_type=MESH,
        )

    def partial_copy(sweep, k):
        return pltpu.make_async_remote_copy(
            src_ref=partial.at[sweep],
            dst_ref=others.at[sweep, k - 1],
            send_sem=sp_sem.at[sweep, k - 1],
            recv_sem=rp_sem.at[sweep, k - 1],
            device_id={"units": lax.rem(unit + k, n_units)},
            device_id_type=MESH,
        )

    def put_first(sweep, c, link, up, down):
        send_first[sweep, c, 0:ROW, :] = link[0:ROW]
        send_first[sweep, c, ROW : ROW + WIN, :] = up[0:WIN]
        send_first[sweep, c, ROW + WIN : FIRST, :] = down[0:WIN]

    for i in (B, M, N):
        loads[i].wait()

    def turn_duals(c, carry):
        link, up, down = (inbuf[i, rows_of(c), :].T for i in (B, M, N))
        state[B, c] = link
        state[M, c] = up
        state[N, c] = down
        put_first(0, c, link, up, down)
        return carry

    for c in range(chunks):
        turn_duals(c, 0)
    pl.semaphore_wait(barrier, n_all - 1)

    def send_duals(c, carry):
        first_copy(0, c).start()
        return carry

    for c in range(chunks):
        send_duals(c, 0)
    for load in unit_loads:
        load.wait()
    for c in range(chunks):
        part = pl.ds(c * LANES, LANES)
        ipar[c, 0:1, :] = up_window[part].reshape(1, LANES)
        ipar[c, 1:2, :] = down_window[part].reshape(1, LANES)
        ipar[c, 2:3, :] = unit_zone[part].reshape(1, LANES)
        limit = capacity[part].reshape(1, LANES)
        fpar[c, 0:1, :] = limit
        fpar[c, 1:2, :] = 1.0 / (1.0 + limit * limit)
        fpar[c, 2:3, :] = jnp.where(switchable[part].reshape(1, LANES) == 0, 2.0, -3e38)
        fpar[c, 3:4, :] = fixed_cost[part].reshape(1, LANES)
        fpar[c, 4:5, :] = start_cost[part].reshape(1, LANES)
        rank = lax.broadcasted_iota(jnp.int32, (zones, LANES), 0)
        hit = rank == jnp.broadcast_to(ipar[c, 2:3, :], (zones, LANES))
        onehot = jnp.where(hit, 1.0, 0.0).astype(jnp.bfloat16)
        onehots[c, 0:zones, :] = onehot
        onehots[c, zones:, :] = onehot
    for i in (C, S, G, F):
        loads[i].wait()

    def turn_rest(c, carry):
        for i in (C, G, S, F):
            state[i, c] = inbuf[i, rows_of(c), :].T
        return carry

    for c in range(chunks):
        turn_rest(c, 0)
    price_load.wait()
    demand_load.wait()
    change[...] = jnp.zeros_like(change)

    def spread_price():
        price_parts[...] = two_parts(price_v[...].T)
        for c in range(chunks):
            spread[c] = jnp.dot(price_parts[...], onehots[c], preferred_element_type=jnp.float32)

    def gather_output(sweep):
        total = None
        for c in range(chunks):
            onehot = onehots[c, 0:zones, :]
            term = lax.dot_general(
                jnp.concatenate([onehot, onehot], axis=1),
                output_parts[c],
                (((1,), (1,)), ((), ())),
                preferred_element_type=jnp.float32,
            )
            total = term if total is None else total + term
        partial[sweep] = total

    def adjoint(sweep, c, carry):
        first_copy(sweep, c).wait_recv()
        link, up, down = (state[i, c] for i in (B, M, N))
        rim = halo_first.at[sweep, c]
        long = (span + WIN, LANES)
        up_bits = bits_of(ipar[c, 0:1, :], long)
        down_bits = bits_of(ipar[c, 1:2, :], long)
        up_long = jnp.concatenate([up, rim[ROW : ROW + WIN, :]], axis=0)
        total = windowed(doubled(up_long, sooner), up_bits, sooner)[:span] - link
        down_long = jnp.concatenate([down, rim[ROW + WIN : FIRST, :]], axis=0)
        total = total + windowed(doubled(down_long, sooner), down_bits, sooner)[:span]
        grads[1, c] = total
        lagged = down_long
        for b in range(BITS):
            lagged = jnp.where(down_bits[b], sooner(lagged, 1 << b), lagged)
        link_long = jnp.concatenate([link, rim[0:ROW, :]], axis=0)
        grads[0, c] = link - sooner(link_long, 1)[:span] - up + lagged[:span]
        return carry

    def primal(sweep, step, c, carry):
        limit = fpar[c, 0:1, :]
        commit, output, startup = (state[i, c] for i in (C, G, S))
        point_x = commit - step * (fpar[c, 3:4, :] + grads[0, c])
        point_g = output - step * (state[F, c] + spread[c])
        point_x = jnp.maximum(point_x, fpar[c, 2:3, :])
        above = point_g > limit * point_x
        ratio = jnp.clip((point_x + limit * point_g) * fpar[c, 1:2, :], 0.0, 1.0)
        new_commit = jnp.where(above, ratio, jnp.clip(point_x, 0.0, 1.0))
        new_output = jnp.where(above, limit * ratio, jnp.minimum(jnp.maximum(point_g, 0.0), limit))
        new_startup = jnp.clip(startup - step * (fpar[c, 4:5, :] + grads[1, c]), 0.0, 1.0)
        reflect_commit = 2.0 * new_commit - commit
        reflect_startup = 2.0 * new_startup - startup
        output_parts[c] = two_parts(2.0 * new_output - output)
        reflect[0, c] = reflect_commit
        reflect[1, c] = reflect_startup
        send_last[sweep, c, 0:WIN, :] = reflect_commit[span - WIN :]
        send_last[sweep, c, WIN:, :] = reflect_startup[span - WIN :]
        last_copy(sweep, c).start()
        if sweep == 0:
            change[0:ROW, :] += (
                tile_sum(jnp.square(new_commit - commit))
                + tile_sum(jnp.square(new_output - output))
                + tile_sum(jnp.square(new_startup - startup))
            )
            state[C, c] = new_commit
            state[G, c] = new_output
            state[S, c] = new_startup
        else:
            give(0, c, new_commit)
            give(1, c, new_output)
            give(2, c, new_startup)
        return carry

    def store_of(i, c):
        return pltpu.make_async_copy(turned.at[i, c], turned_hbm.at[i, c], out_sem.at[i, c])

    def give(i, c, value):
        turned[i, c] = value
        store_of(i, c).start()

    def rows(sweep, step, c, carry):
        last_copy(sweep, c).wait_recv()
        rim = halo_last.at[sweep, c]
        commit, startup = reflect[0, c], reflect[1, c]
        commit_long = jnp.concatenate([rim[0:WIN, :], commit], axis=0)
        startup_long = jnp.concatenate([rim[WIN:, :], startup], axis=0)
        long = (span + WIN, LANES)
        up_bits = bits_of(ipar[c, 0:1, :], long)
        down_bits = bits_of(ipar[c, 1:2, :], long)
        sums = doubled(startup_long, later)
        upper = windowed(sums, up_bits, later)[WIN:] - commit
        lower = windowed(sums, down_bits, later, commit_long)[WIN:] - 1.0
        link = commit - later(commit_long, 1)[WIN:] - startup
        olds = tuple(state[i, c] for i in (B, M, N))
        news = tuple(
            jnp.maximum(old + step * row, 0.0) for old, row in zip(olds, (link, upper, lower))
        )
        if sweep == 0:
            put_first(1, c, *news)
            first_copy(1, c).start()
            squares = [tile_sum(jnp.square(new - old)) for new, old in zip(news, olds)]
            change[ROW:, :] += squares[0] + squares[1] + squares[2]
            for i, new in zip((B, M, N), news):
                state[i, c] = new
        else:
            for i, new in enumerate(news):
                give(3 + i, c, new)
        return carry

    def totals(sweep):
        total = partial[sweep]
        for k in range(1, n_units):
            partial_copy(sweep, k).wait_recv()
            total = total + others[sweep, k - 1]
        return total

    def weight_copy(k):
        peer = lax.rem(me + k, n_all)
        return pltpu.make_async_remote_copy(
            src_ref=slots.at[me],
            dst_ref=slots.at[me],
            send_sem=sw_sem.at[k],
            recv_sem=rw_sem.at[me],
            device_id={"hours": peer // n_units, "units": lax.rem(peer, n_units)},
            device_id_type=MESH,
        )

    def weight_arrival(k):
        peer = lax.rem(me + k, n_all)
        return pltpu.make_async_remote_copy(
            src_ref=slots.at[peer],
            dst_ref=slots.at[peer],
            send_sem=sw_sem.at[k],
            recv_sem=rw_sem.at[peer],
            device_id={"hours": peer // n_units, "units": lax.rem(peer, n_units)},
            device_id_type=MESH,
        )

    primal_step = step_scale
    dual_step = step_scale
    for sweep in range(2):
        spread_price()
        if sweep == 0:

            def both(c, carry):
                adjoint(0, c, 0)
                return primal(0, step_scale, c, carry)

            lax.fori_loop(0, chunks, both, 0)
        else:
            lax.fori_loop(0, chunks, functools.partial(adjoint, 1), 0)

            def send_done(k, carry):
                weight_arrival(k).wait_recv()
                return carry

            lax.fori_loop(1, n_all, send_done, 0)
            summed = jnp.sum(slots[...], axis=0)
            primal_change = jnp.sum(summed[:ROW], keepdims=True)
            dual_change = jnp.sum(summed[ROW:], keepdims=True)
            weight = jnp.sqrt(jnp.sqrt((dual_change + epsilon) / (primal_change + epsilon)))
            primal_step = jnp.broadcast_to(step_scale / weight, (1, LANES))
            dual_step = jnp.broadcast_to(step_scale * weight, (1, LANES))
            lax.fori_loop(0, chunks, functools.partial(primal, 1, primal_step), 0)
        gather_output(sweep)
        for k in range(1, n_units):
            partial_copy(sweep, k).start()
        lax.fori_loop(0, chunks, functools.partial(rows, sweep, dual_step), 0)
        price = price_v[...]
        new_price = price + dual_step * (totals(sweep) - demand_v[...])
        price_v[...] = new_price
        if sweep == 0:
            change[ROW:, :] += tile_sum(jnp.square(new_price - price)) * (1.0 / n_units)
            slots[me] = change[...]

            def send_weight(k, carry):
                weight_copy(k).start()
                return carry

            lax.fori_loop(1, n_all, send_weight, 0)


    price_store = pltpu.make_async_copy(price_v, price_res, price_sem)
    price_store.start()

    def finish(c, carry):
        for sweep in range(2):
            first_copy(sweep, c).wait_send()
            last_copy(sweep, c).wait_send()
        for i in range(6):
            store_of(i, c).wait()
        return carry

    lax.fori_loop(0, chunks, finish, 0)
    for sweep in range(2):
        for k in range(1, n_units):
            partial_copy(sweep, k).wait_send()

    def finish_weight(k, carry):
        weight_copy(k).wait_send()
        return carry

    lax.fori_loop(1, n_all, finish_weight, 0)
    price_store.wait()


def place(turned, price, *rest):
    results, price_res, held, outbuf, load_sem, sem, price_sem = rest[:6], *rest[6:]
    chunks = turned.shape[1]
    loads = [pltpu.make_async_copy(turned.at[i], held.at[i], load_sem.at[i]) for i in range(6)]
    stores = [pltpu.make_async_copy(outbuf.at[i], results[i], sem.at[i]) for i in range(6)]
    for load in loads:
        load.start()
    price_store = pltpu.make_async_copy(price, price_res, price_sem)
    price_store.start()
    for i in range(6):
        loads[i].wait()
        for c in range(chunks):
            outbuf[i, c * LANES : (c + 1) * LANES, :] = held[i, c].T
        stores[i].start()
    for store in stores:
        store.wait()
    price_store.wait()


def body(*args):
    n_hours = lax.axis_size("hours")
    n_units = lax.axis_size("units")
    n_all = n_hours * n_units
    fuel_cost, demand = args[7], args[8]
    units, span = fuel_cost.shape
    zones = demand.shape[0]
    chunks = units // LANES
    f32 = jnp.float32
    wide = jax.ShapeDtypeStruct((units, span), f32)
    small = jax.ShapeDtypeStruct((zones, span), f32)
    hbm = pl.BlockSpec(memory_space=pltpu.HBM)
    dma = pltpu.SemaphoreType.DMA
    peers = max(n_units - 1, 1)
    turned, price = pl.pallas_call(
        functools.partial(kernel, n_hours, n_units),
        out_shape=(jax.ShapeDtypeStruct((6, chunks, span, LANES), f32), small),
        in_specs=[hbm] * 16,
        out_specs=[hbm] * 2,
        scratch_shapes=[
            *[pltpu.VMEM((units,), arg.dtype) for arg in args[:7]],
            pltpu.VMEM((7, units, span), f32),
            pltpu.VMEM((6, chunks, span, LANES), f32),
            pltpu.VMEM((zones, span), f32),
            pltpu.VMEM((span, 2 * zones), jnp.bfloat16),
            pltpu.VMEM((chunks, 2 * zones, LANES), jnp.bfloat16),
            pltpu.VMEM((chunks, span, LANES), f32),
            pltpu.VMEM((chunks, span, 2 * LANES), jnp.bfloat16),
            pltpu.VMEM((zones, span), f32),
            pltpu.VMEM((chunks, ROW, LANES), jnp.int32),
            pltpu.VMEM((chunks, ROW, LANES), f32),
            pltpu.VMEM((7, chunks, span, LANES), f32),
            pltpu.VMEM((2, chunks, span, LANES), f32),
            pltpu.VMEM((2, chunks, span, LANES), f32),
            pltpu.VMEM((2, chunks, FIRST, LANES), f32),
            pltpu.VMEM((2, chunks, FIRST, LANES), f32),
            pltpu.VMEM((2, chunks, 2 * WIN, LANES), f32),
            pltpu.VMEM((2, chunks, 2 * WIN, LANES), f32),
            pltpu.VMEM((2, zones, span), f32),
            pltpu.VMEM((2, peers, zones, span), f32),
            pltpu.VMEM((2 * ROW, LANES), f32),
            pltpu.VMEM((n_all, 2 * ROW, LANES), f32),
            dma((7,)),
            dma((2,)),
            dma((7,)),
            dma((6, chunks)),
            dma,
            dma((2, chunks)),
            dma((2, chunks)),
            dma((2, chunks)),
            dma((2, chunks)),
            dma((2, peers)),
            dma((2, peers)),
            dma((n_all,)),
            dma((n_all,)),
        ],
        compiler_params=pltpu.CompilerParams(
            collective_id=0, has_side_effects=True, vmem_limit_bytes=56 * 1024 * 1024
        ),
    )(*args)
    commit, output, startup, link, up, down, price = pl.pallas_call(
        place,
        out_shape=(wide,) * 6 + (small,),
        in_specs=[hbm] * 2,
        out_specs=[hbm] * 7,
        scratch_shapes=[
            pltpu.VMEM((6, chunks, span, LANES), f32),
            pltpu.VMEM((6, units, span), f32),
            dma((6,)),
            dma((6,)),
            dma,
        ],
        compiler_params=pltpu.CompilerParams(vmem_limit_bytes=56 * 1024 * 1024),
    )(turned, price)
    return (commit, output, startup, price, link, up, down)


def solution(mesh):
    unit = P("units")
    wide = P(("groups", "units"), "hours")
    zonal = P("groups", "hours")
    return jax.shard_map(
        body,
        mesh=mesh,
        in_specs=(unit,) * 7 + (wide, zonal, wide, wide, wide, zonal, wide, wide, wide),
        out_specs=(wide, wide, wide, zonal, wide, wide, wide),
        check_vma=False,
    )
```

```python
import functools

import jax
import jax.numpy as jnp
from jax import lax
from jax.experimental import pallas as pl
from jax.experimental.pallas import tpu as pltpu
from jax.sharding import PartitionSpec as P

WIN = 24
BITS = 5
LANES = 128
ROW = 8
FIRST = ROW + 2 * WIN

step_scale = 0.015
epsilon = 1e-06

MESH = pl.DeviceIdType.MESH


def later(x, k):
    return pltpu.roll(x, k, 0)


def sooner(x, k):
    return pltpu.roll(x, x.shape[0] - k, 0)


def bits_of(window, shape):
    wide = jnp.broadcast_to(window, shape)
    return [(wide & (1 << b)) != 0 for b in range(BITS)]


def doubled(x, move):
    sums = [x]
    for b in range(BITS - 1):
        sums.append(sums[-1] + move(sums[-1], 1 << b))
    return sums


def windowed(sums, bits, move, beyond=None):
    if beyond is None:
        total = jnp.where(bits[0], sums[0], 0.0)
    else:
        total = jnp.where(bits[0], sums[0] + move(beyond, 1), beyond)
    for b in range(1, BITS):
        total = jnp.where(bits[b], sums[b] + move(total, 1 << b), total)
    return total


def tile_sum(x):
    return jnp.sum(x.reshape(-1, ROW, x.shape[1]), axis=0)


def two_parts(values):
    high = values.astype(jnp.bfloat16)
    low = (values - high.astype(jnp.float32)).astype(jnp.bfloat16)
    return jnp.concatenate([high, low], axis=1)


def kernel(
    n_hours,
    n_units,
    unit_zone_hbm,
    up_window_hbm,
    down_window_hbm,
    switchable_hbm,
    capacity_hbm,
    fixed_cost_hbm,
    start_cost_hbm,
    fuel_hbm,
    demand_hbm,
    commit_hbm,
    output_hbm,
    startup_hbm,
    price_hbm,
    link_hbm,
    up_hbm,
    down_hbm,
    turned_hbm,
    price_res,
    unit_zone,
    up_window,
    down_window,
    switchable,
    capacity,
    fixed_cost,
    start_cost,
    inbuf,
    turned,
    price_v,
    price_parts,
    onehots,
    spread,
    output_parts,
    demand_v,
    ipar,
    fpar,
    state,
    reflect,
    grads,
    send_first,
    halo_first,
    send_last,
    halo_last,
    partial,
    others,
    change,
    slots,
    in_sem,
    small_sem,
    unit_sem,
    out_sem,
    price_sem,
    sf_sem,
    rf_sem,
    sl_sem,
    rl_sem,
    sp_sem,
    rp_sem,
    sw_sem,
    rw_sem,
):
    hour = lax.axis_index("hours")
    unit = lax.axis_index("units")
    me = hour * n_units + unit
    n_all = n_hours * n_units
    following = lax.rem(hour + 1, n_hours)
    preceding = lax.rem(hour + n_hours - 1, n_hours)
    chunks = state.shape[1]
    span = state.shape[2]
    zones = price_v.shape[0]
    C, G, S, F, B, M, N = range(7)

    sources = (commit_hbm, output_hbm, startup_hbm, fuel_hbm, link_hbm, up_hbm, down_hbm)
    loads = [pltpu.make_async_copy(src, inbuf.at[i], in_sem.at[i]) for i, src in enumerate(sources)]
    price_load = pltpu.make_async_copy(price_hbm, price_v, small_sem.at[0])
    demand_load = pltpu.make_async_copy(demand_hbm, demand_v, small_sem.at[1])
    unit_pairs = (
        (unit_zone_hbm, unit_zone),
        (up_window_hbm, up_window),
        (down_window_hbm, down_window),
        (switchable_hbm, switchable),
        (capacity_hbm, capacity),
        (fixed_cost_hbm, fixed_cost),
        (start_cost_hbm, start_cost),
    )
    unit_loads = [
        pltpu.make_async_copy(src, dst, unit_sem.at[i]) for i, (src, dst) in enumerate(unit_pairs)
    ]
    for i in (B, M, N):
        loads[i].start()
    for load in unit_loads:
        load.start()
    for i in (C, S, G, F):
        loads[i].start()
    price_load.start()
    demand_load.start()

    barrier = pltpu.get_barrier_semaphore()

    def greet(k, carry):
        peer = lax.rem(me + k, n_all)
        pl.semaphore_signal(
            barrier,
            inc=1,
            device_id={"hours": peer // n_units, "units": lax.rem(peer, n_units)},
            device_id_type=MESH,
        )
        return carry

    lax.fori_loop(1, n_all, greet, 0)

    def rows_of(c):
        return pl.ds(c * LANES, LANES)

    def first_copy(sweep, c):
        return pltpu.make_async_remote_copy(
            src_ref=send_first.at[sweep, c],
            dst_ref=halo_first.at[sweep, c],
            send_sem=sf_sem.at[sweep, c],
            recv_sem=rf_sem.at[sweep, c],
            device_id={"hours": preceding},
            device_id_type=MESH,
        )

    def last_copy(sweep, c):
        return pltpu.make_async_remote_copy(
            src_ref=send_last.at[sweep, c],
            dst_ref=halo_last.at[sweep, c],
            send_sem=sl_sem.at[sweep, c],
            recv_sem=rl_sem.at[sweep, c],
            device_id={"hours": following},
            device_id_type=MESH,
        )

    def partial_copy(sweep, k):
        return pltpu.make_async_remote_copy(
            src_ref=partial.at[sweep],
            dst_ref=others.at[sweep, k - 1],
            send_sem=sp_sem.at[sweep, k - 1],
            recv_sem=rp_sem.at[sweep, k - 1],
            device_id={"units": lax.rem(unit + k, n_units)},
            device_id_type=MESH,
        )

    def put_first(sweep, c, link, up, down):
        send_first[sweep, c, 0:ROW, :] = link[0:ROW]
        send_first[sweep, c, ROW : ROW + WIN, :] = up[0:WIN]
        send_first[sweep, c, ROW + WIN : FIRST, :] = down[0:WIN]

    for i in (B, M, N):
        loads[i].wait()

    def turn_duals(c, carry):
        link, up, down = (inbuf[i, rows_of(c), :].T for i in (B, M, N))
        state[B, c] = link
        state[M, c] = up
        state[N, c] = down
        put_first(0, c, link, up, down)
        return carry

    for c in range(chunks):
        turn_duals(c, 0)
    pl.semaphore_wait(barrier, n_all - 1)

    def send_duals(c, carry):
        first_copy(0, c).start()
        return carry

    for c in range(chunks):
        send_duals(c, 0)
    for load in unit_loads:
        load.wait()
    for c in range(chunks):
        part = pl.ds(c * LANES, LANES)
        ipar[c, 0:1, :] = up_window[part].reshape(1, LANES)
        ipar[c, 1:2, :] = down_window[part].reshape(1, LANES)
        ipar[c, 2:3, :] = unit_zone[part].reshape(1, LANES)
        limit = capacity[part].reshape(1, LANES)
        fpar[c, 0:1, :] = limit
        fpar[c, 1:2, :] = 1.0 / (1.0 + limit * limit)
        fpar[c, 2:3, :] = jnp.where(switchable[part].reshape(1, LANES) == 0, 2.0, -3e38)
        fpar[c, 3:4, :] = fixed_cost[part].reshape(1, LANES)
        fpar[c, 4:5, :] = start_cost[part].reshape(1, LANES)
        rank = lax.broadcasted_iota(jnp.int32, (zones, LANES), 0)
        hit = rank == jnp.broadcast_to(ipar[c, 2:3, :], (zones, LANES))
        onehot = jnp.where(hit, 1.0, 0.0).astype(jnp.bfloat16)
        onehots[c, 0:zones, :] = onehot
        onehots[c, zones:, :] = onehot
    for i in (C, S, G, F):
        loads[i].wait()

    def turn_rest(c, carry):
        for i in (C, G, S, F):
            state[i, c] = inbuf[i, rows_of(c), :].T
        return carry

    for c in range(chunks):
        turn_rest(c, 0)
    price_load.wait()
    demand_load.wait()
    change[...] = jnp.zeros_like(change)

    def spread_price():
        price_parts[...] = two_parts(price_v[...].T)
        for c in range(chunks):
            spread[c] = jnp.dot(price_parts[...], onehots[c], preferred_element_type=jnp.float32)

    def gather_output(sweep):
        total = None
        for c in range(chunks):
            onehot = onehots[c, 0:zones, :]
            term = lax.dot_general(
                jnp.concatenate([onehot, onehot], axis=1),
                output_parts[c],
                (((1,), (1,)), ((), ())),
                preferred_element_type=jnp.float32,
            )
            total = term if total is None else total + term
        partial[sweep] = total

    def adjoint(sweep, c, carry):
        first_copy(sweep, c).wait_recv()
        link, up, down = (state[i, c] for i in (B, M, N))
        rim = halo_first.at[sweep, c]
        long = (span + WIN, LANES)
        up_bits = bits_of(ipar[c, 0:1, :], long)
        down_bits = bits_of(ipar[c, 1:2, :], long)
        up_long = jnp.concatenate([up, rim[ROW : ROW + WIN, :]], axis=0)
        total = windowed(doubled(up_long, sooner), up_bits, sooner)[:span] - link
        down_long = jnp.concatenate([down, rim[ROW + WIN : FIRST, :]], axis=0)
        total = total + windowed(doubled(down_long, sooner), down_bits, sooner)[:span]
        grads[1, c] = total
        lagged = down_long
        for b in range(BITS):
            lagged = jnp.where(down_bits[b], sooner(lagged, 1 << b), lagged)
        link_long = jnp.concatenate([link, rim[0:ROW, :]], axis=0)
        grads[0, c] = link - sooner(link_long, 1)[:span] - up + lagged[:span]
        return carry

    def primal(sweep, step, c, carry):
        limit = fpar[c, 0:1, :]
        commit, output, startup = (state[i, c] for i in (C, G, S))
        point_x = commit - step * (fpar[c, 3:4, :] + grads[0, c])
        point_g = output - step * (state[F, c] + spread[c])
        point_x = jnp.maximum(point_x, fpar[c, 2:3, :])
        above = point_g > limit * point_x
        ratio = jnp.clip((point_x + limit * point_g) * fpar[c, 1:2, :], 0.0, 1.0)
        new_commit = jnp.where(above, ratio, jnp.clip(point_x, 0.0, 1.0))
        new_output = jnp.where(above, limit * ratio, jnp.minimum(jnp.maximum(point_g, 0.0), limit))
        new_startup = jnp.clip(startup - step * (fpar[c, 4:5, :] + grads[1, c]), 0.0, 1.0)
        reflect_commit = 2.0 * new_commit - commit
        reflect_startup = 2.0 * new_startup - startup
        output_parts[c] = two_parts(2.0 * new_output - output)
        reflect[0, c] = reflect_commit
        reflect[1, c] = reflect_startup
        send_last[sweep, c, 0:WIN, :] = reflect_commit[span - WIN :]
        send_last[sweep, c, WIN:, :] = reflect_startup[span - WIN :]
        last_copy(sweep, c).start()
        if sweep == 0:
            change[0:ROW, :] += (
                tile_sum(jnp.square(new_commit - commit))
                + tile_sum(jnp.square(new_output - output))
                + tile_sum(jnp.square(new_startup - startup))
            )
            state[C, c] = new_commit
            state[G, c] = new_output
            state[S, c] = new_startup
        else:
            give(0, c, new_commit)
            give(1, c, new_output)
            give(2, c, new_startup)
        return carry

    def store_of(i, c):
        return pltpu.make_async_copy(turned.at[i, c], turned_hbm.at[i, c], out_sem.at[i, c])

    def give(i, c, value):
        turned[i, c] = value
        store_of(i, c).start()

    def rows(sweep, step, c, carry):
        last_copy(sweep, c).wait_recv()
        rim = halo_last.at[sweep, c]
        commit, startup = reflect[0, c], reflect[1, c]
        commit_long = jnp.concatenate([rim[0:WIN, :], commit], axis=0)
        startup_long = jnp.concatenate([rim[WIN:, :], startup], axis=0)
        long = (span + WIN, LANES)
        up_bits = bits_of(ipar[c, 0:1, :], long)
        down_bits = bits_of(ipar[c, 1:2, :], long)
        sums = doubled(startup_long, later)
        upper = windowed(sums, up_bits, later)[WIN:] - commit
        lower = windowed(sums, down_bits, later, commit_long)[WIN:] - 1.0
        link = commit - later(commit_long, 1)[WIN:] - startup
        olds = tuple(state[i, c] for i in (B, M, N))
        news = tuple(
            jnp.maximum(old + step * row, 0.0) for old, row in zip(olds, (link, upper, lower))
        )
        if sweep == 0:
            put_first(1, c, *news)
            first_copy(1, c).start()
            squares = [tile_sum(jnp.square(new - old)) for new, old in zip(news, olds)]
            change[ROW:, :] += squares[0] + squares[1] + squares[2]
            for i, new in zip((B, M, N), news):
                state[i, c] = new
        else:
            for i, new in enumerate(news):
                give(3 + i, c, new)
        return carry

    def totals(sweep):
        total = partial[sweep]
        for k in range(1, n_units):
            partial_copy(sweep, k).wait_recv()
            total = total + others[sweep, k - 1]
        return total

    def weight_copy(k):
        peer = lax.rem(me + k, n_all)
        return pltpu.make_async_remote_copy(
            src_ref=slots.at[me],
            dst_ref=slots.at[me],
            send_sem=sw_sem.at[k],
            recv_sem=rw_sem.at[me],
            device_id={"hours": peer // n_units, "units": lax.rem(peer, n_units)},
            device_id_type=MESH,
        )

    def weight_arrival(k):
        peer = lax.rem(me + k, n_all)
        return pltpu.make_async_remote_copy(
            src_ref=slots.at[peer],
            dst_ref=slots.at[peer],
            send_sem=sw_sem.at[k],
            recv_sem=rw_sem.at[peer],
            device_id={"hours": peer // n_units, "units": lax.rem(peer, n_units)},
            device_id_type=MESH,
        )

    primal_step = step_scale
    dual_step = step_scale
    for sweep in range(2):
        spread_price()
        if sweep == 0:

            def both(c, carry):
                adjoint(0, c, 0)
                return primal(0, step_scale, c, carry)

            lax.fori_loop(0, chunks, both, 0)
        else:
            lax.fori_loop(0, chunks, functools.partial(adjoint, 1), 0)

            def send_done(k, carry):
                weight_arrival(k).wait_recv()
                return carry

            lax.fori_loop(1, n_all, send_done, 0)
            summed = jnp.sum(slots[...], axis=0)
            primal_change = jnp.sum(summed[0:1], keepdims=True)
            dual_change = jnp.sum(summed[1:2], keepdims=True)
            weight = jnp.sqrt(jnp.sqrt((dual_change + epsilon) / (primal_change + epsilon)))
            primal_step = jnp.broadcast_to(step_scale / weight, (1, LANES))
            dual_step = jnp.broadcast_to(step_scale * weight, (1, LANES))
            lax.fori_loop(0, chunks, functools.partial(primal, 1, primal_step), 0)
        gather_output(sweep)
        for k in range(1, n_units):
            partial_copy(sweep, k).start()
        lax.fori_loop(0, chunks, functools.partial(rows, sweep, dual_step), 0)
        price = price_v[...]
        new_price = price + dual_step * (totals(sweep) - demand_v[...])
        price_v[...] = new_price
        if sweep == 0:
            change[ROW:, :] += tile_sum(jnp.square(new_price - price)) * (1.0 / n_units)
            slots[me, 0:1, :] = jnp.sum(change[:ROW, :], axis=0, keepdims=True)
            slots[me, 1:2, :] = jnp.sum(change[ROW:, :], axis=0, keepdims=True)

            def send_weight(k, carry):
                weight_copy(k).start()
                return carry

            lax.fori_loop(1, n_all, send_weight, 0)


    price_store = pltpu.make_async_copy(price_v, price_res, price_sem)
    price_store.start()

    def finish(c, carry):
        for sweep in range(2):
            first_copy(sweep, c).wait_send()
            last_copy(sweep, c).wait_send()
        for i in range(6):
            store_of(i, c).wait()
        return carry

    lax.fori_loop(0, chunks, finish, 0)
    for sweep in range(2):
        for k in range(1, n_units):
            partial_copy(sweep, k).wait_send()

    def finish_weight(k, carry):
        weight_copy(k).wait_send()
        return carry

    lax.fori_loop(1, n_all, finish_weight, 0)
    price_store.wait()


def place(turned, price, *rest):
    results, price_res, held, outbuf, load_sem, sem, price_sem = rest[:6], *rest[6:]
    chunks = turned.shape[1]
    loads = [pltpu.make_async_copy(turned.at[i], held.at[i], load_sem.at[i]) for i in range(6)]
    stores = [pltpu.make_async_copy(outbuf.at[i], results[i], sem.at[i]) for i in range(6)]
    for load in loads:
        load.start()
    price_store = pltpu.make_async_copy(price, price_res, price_sem)
    price_store.start()
    for i in range(6):
        loads[i].wait()
        for c in range(chunks):
            outbuf[i, c * LANES : (c + 1) * LANES, :] = held[i, c].T
        stores[i].start()
    for store in stores:
        store.wait()
    price_store.wait()


def body(*args):
    n_hours = lax.axis_size("hours")
    n_units = lax.axis_size("units")
    n_all = n_hours * n_units
    fuel_cost, demand = args[7], args[8]
    units, span = fuel_cost.shape
    zones = demand.shape[0]
    chunks = units // LANES
    f32 = jnp.float32
    wide = jax.ShapeDtypeStruct((units, span), f32)
    small = jax.ShapeDtypeStruct((zones, span), f32)
    hbm = pl.BlockSpec(memory_space=pltpu.HBM)
    dma = pltpu.SemaphoreType.DMA
    peers = max(n_units - 1, 1)
    turned, price = pl.pallas_call(
        functools.partial(kernel, n_hours, n_units),
        out_shape=(jax.ShapeDtypeStruct((6, chunks, span, LANES), f32), small),
        in_specs=[hbm] * 16,
        out_specs=[hbm] * 2,
        scratch_shapes=[
            *[pltpu.VMEM((units,), arg.dtype) for arg in args[:7]],
            pltpu.VMEM((7, units, span), f32),
            pltpu.VMEM((6, chunks, span, LANES), f32),
            pltpu.VMEM((zones, span), f32),
            pltpu.VMEM((span, 2 * zones), jnp.bfloat16),
            pltpu.VMEM((chunks, 2 * zones, LANES), jnp.bfloat16),
            pltpu.VMEM((chunks, span, LANES), f32),
            pltpu.VMEM((chunks, span, 2 * LANES), jnp.bfloat16),
            pltpu.VMEM((zones, span), f32),
            pltpu.VMEM((chunks, ROW, LANES), jnp.int32),
            pltpu.VMEM((chunks, ROW, LANES), f32),
            pltpu.VMEM((7, chunks, span, LANES), f32),
            pltpu.VMEM((2, chunks, span, LANES), f32),
            pltpu.VMEM((2, chunks, span, LANES), f32),
            pltpu.VMEM((2, chunks, FIRST, LANES), f32),
            pltpu.VMEM((2, chunks, FIRST, LANES), f32),
            pltpu.VMEM((2, chunks, 2 * WIN, LANES), f32),
            pltpu.VMEM((2, chunks, 2 * WIN, LANES), f32),
            pltpu.VMEM((2, zones, span), f32),
            pltpu.VMEM((2, peers, zones, span), f32),
            pltpu.VMEM((2 * ROW, LANES), f32),
            pltpu.VMEM((n_all, 2, LANES), f32),
            dma((7,)),
            dma((2,)),
            dma((7,)),
            dma((6, chunks)),
            dma,
            dma((2, chunks)),
            dma((2, chunks)),
            dma((2, chunks)),
            dma((2, chunks)),
            dma((2, peers)),
            dma((2, peers)),
            dma((n_all,)),
            dma((n_all,)),
        ],
        compiler_params=pltpu.CompilerParams(
            collective_id=0, has_side_effects=True, vmem_limit_bytes=56 * 1024 * 1024
        ),
    )(*args)
    commit, output, startup, link, up, down, price = pl.pallas_call(
        place,
        out_shape=(wide,) * 6 + (small,),
        in_specs=[hbm] * 2,
        out_specs=[hbm] * 7,
        scratch_shapes=[
            pltpu.VMEM((6, chunks, span, LANES), f32),
            pltpu.VMEM((6, units, span), f32),
            dma((6,)),
            dma((6,)),
            dma,
        ],
        compiler_params=pltpu.CompilerParams(vmem_limit_bytes=56 * 1024 * 1024),
    )(turned, price)
    return (commit, output, startup, price, link, up, down)


def solution(mesh):
    unit = P("units")
    wide = P(("groups", "units"), "hours")
    zonal = P("groups", "hours")
    return jax.shard_map(
        body,
        mesh=mesh,
        in_specs=(unit,) * 7 + (wide, zonal, wide, wide, wide, zonal, wide, wide, wide),
        out_specs=(wide, wide, wide, zonal, wide, wide, wide),
        check_vma=False,
    )
```
